32 devices in a mesh: dp: 4 (over y, x), tensor: 8 (over z, core).
Axes of the slice: x: 2, y: 2, z: 4, core: 2. Of those that a mesh axis runs over, the one named last changes fastest.
Arguments:
- tokens_in: bfloat16 [2048, 128, 128], P('dp', 'tensor'), may hold values from -6 to 6
- right_one: bfloat16 [128, 128, 128], P('tensor'), may hold values from -0.5 to 0.5
- left_one: bfloat16 [128, 128, 128], P('tensor'), may hold values from -0.5 to 0.5
- right_two: bfloat16 [128, 128, 128], P('tensor'), may hold values from -0.5 to 0.5
- left_two: bfloat16 [128, 128, 128], P('tensor'), may hold values from -0.5 to 0.5
- out_grad: bfloat16 [2048, 128, 128], P('dp', 'tensor'), may hold values from -6 to 6
Outputs:
- layer_out: bfloat16 [2048, 128, 128], P('dp', 'tensor')
- input_grad: bfloat16 [2048, 128, 128], P('dp', 'tensor')
- grad_right_one: float32 [128, 128, 128], P('tensor', 'dp')
- grad_left_one: float32 [128, 128, 128], P('tensor', 'dp')
- grad_right_two: float32 [128, 128, 128], P('tensor', 'dp')
- grad_left_two: float32 [128, 128, 128], P('tensor', 'dp')
The draws below stay inside these ranges and needn't reach their ends.
All inputs are finite; a program needn't handle non-finite values.
Results may differ from the reference program's by a relative error of at most 0.0067.
Values may be sent and summed in bfloat16 or wider, within the bound.
A program may use at most 64 MiB of HBM per device.

```python
import math
import jax
import jax.numpy as jnp
from jax import lax

BS = 128
NBLK = 128
TOKENS = 2048


def block_scale(own_key, shape, shards, least, largest):
    gain = 1.0
    for dim, parts in shards:
        steps = jax.random.uniform(jax.random.fold_in(jax.random.fold_in(own_key, 6), dim), (parts,), jnp.float32, least / len(shards), largest / len(shards))
        gain = gain * jnp.repeat(jnp.exp(steps), shape[dim] // parts).reshape((-1,) + (1,) * (len(shape) - 1 - dim))
    return gain


def bell_draw(rng, dims, spread, bound, split=(), kind=jnp.bfloat16):
    array = jax.random.normal(rng, dims, jnp.float32) * spread
    if len(split) > 0:
        array = block_scale(rng, dims, split, -0.22, 0.18) * array
    return jnp.clip(array, min=-bound, max=bound).astype(kind)


def setup_inputs(seed: int = 0) -> dict:
    key_list = jax.random.split(jax.random.key(seed), 7)
    return {
        "tokens_in": bell_draw(key_list[0], (TOKENS, NBLK, BS), 1.0, 6.0, ((0, 4), (1, 8))),
        "right_one": bell_draw(key_list[1], (NBLK, BS, BS), BS ** -0.5, 0.5, ((0, 8),)),
        "left_one": bell_draw(key_list[2], (NBLK, BS, BS), BS ** -0.5, 0.5, ((0, 8),)),
        "right_two": bell_draw(key_list[3], (NBLK, BS, BS), BS ** -0.5, 0.5, ((0, 8),)),
        "left_two": bell_draw(key_list[4], (NBLK, BS, BS), BS ** -0.5, 0.5, ((0, 8),)),
        "out_grad": bell_draw(key_list[5], (TOKENS, NBLK, BS), 1.0, 6.0, ((0, 4), (1, 8))),
    }


def gelu_value(z):
    return 0.5 * z * (1.0 + lax.erf(z / math.sqrt(2.0)))

def gelu_slope(z):
    return 0.5 * (1.0 + lax.erf(z / math.sqrt(2.0))) + z * jnp.exp(-0.5 * z * z) / math.sqrt(2.0 * math.pi)

def blockmul(a, w):
    return jnp.einsum('tpq,pqr->tpr', a.astype(jnp.float32), w.astype(jnp.float32))

def transpose_blocks(a):
    return jnp.swapaxes(a, 1, 2)

def one_block(tokens_in, out_grad, right_one, left_one, right_two, left_two):
    bf = jnp.bfloat16
    f32 = jnp.float32
    u1 = blockmul(tokens_in, right_one).astype(bf)
    v1 = transpose_blocks(u1)
    a1 = blockmul(v1, left_one).astype(bf)
    z1 = transpose_blocks(a1)
    hidden = gelu_value(z1.astype(f32)).astype(bf)
    u2 = blockmul(hidden, right_two).astype(bf)
    v2 = transpose_blocks(u2)
    w2 = blockmul(v2, left_two).astype(bf)
    layer_out = (tokens_in.astype(f32) + transpose_blocks(w2).astype(f32)).astype(bf)
    g2 = transpose_blocks(out_grad).astype(f32)
    gl2 = jnp.einsum('tpq,tpr->pqr', v2.astype(f32), g2)
    dv2 = jnp.einsum('tpr,pqr->tpq', g2, left_two.astype(f32)).astype(bf)
    du2 = transpose_blocks(dv2).astype(f32)
    gr2 = jnp.einsum('tpq,tpr->pqr', hidden.astype(f32), du2)
    dh = jnp.einsum('tpr,pqr->tpq', du2, right_two.astype(f32))
    dz1 = (dh * gelu_slope(z1.astype(f32))).astype(bf)
    da1 = transpose_blocks(dz1).astype(f32)
    gl1 = jnp.einsum('tpq,tpr->pqr', v1.astype(f32), da1)
    dv1 = jnp.einsum('tpr,pqr->tpq', da1, left_one.astype(f32)).astype(bf)
    du1 = transpose_blocks(dv1).astype(f32)
    gr1 = jnp.einsum('tpq,tpr->pqr', tokens_in.astype(f32), du1)
    input_grad = (out_grad.astype(f32) + jnp.einsum('tpr,pqr->tpq', du1, right_one.astype(f32))).astype(bf)
    return (layer_out, input_grad, gr1, gl1, gr2, gl2)

def reference(tokens_in, right_one, left_one, right_two, left_two, out_grad):
    rows = math.gcd(TOKENS, 2048)
    count = TOKENS // rows
    xs = tokens_in.reshape(count, rows, NBLK, BS)
    gs = out_grad.reshape(count, rows, NBLK, BS)
    zero = jnp.zeros((NBLK, BS, BS), jnp.float32)

    def step(carry, pair):
        res = one_block(pair[0], pair[1], right_one, left_one, right_two, left_two)
        carry = (carry[0] + res[2], carry[1] + res[3], carry[2] + res[4], carry[3] + res[5])
        return (carry, (res[0], res[1]))
    grads, outs = lax.scan(step, (zero, zero, zero, zero), (xs, gs))
    layer_out = outs[0].reshape(TOKENS, NBLK, BS)
    input_grad = outs[1].reshape(TOKENS, NBLK, BS)
    return (layer_out, input_grad, grads[0], grads[1], grads[2], grads[3])
```

```python
import math

import jax
import jax.numpy as jnp
from jax import lax
from jax.sharding import PartitionSpec as P


def gelu_value(z):
    return 0.5 * z * (1.0 + lax.erf(z / math.sqrt(2.0)))


def gelu_slope(z):
    return 0.5 * (1.0 + lax.erf(z / math.sqrt(2.0))) + z * jnp.exp(-0.5 * z * z) / math.sqrt(
        2.0 * math.pi
    )


def gather_factor(factor, n_dp):
    blocks, rows, cols = factor.shape
    flat = factor.reshape(blocks * rows, cols)
    part = flat.shape[0] // n_dp
    mine = lax.dynamic_slice_in_dim(flat, lax.axis_index("dp") * part, part, axis=0)
    whole = lax.all_gather(mine, ("tensor", "dp"), axis=0, tiled=True)
    return whole.reshape(-1, rows, cols)


def reduce_all(grad):
    grad = lax.psum_scatter(grad.astype(jnp.bfloat16), "dp", scatter_dimension=1, tiled=True)
    return lax.psum_scatter(grad, "tensor", scatter_dimension=0, tiled=True).astype(jnp.float32)


def to_tokens(values):
    return lax.all_to_all(values, "tensor", split_axis=0, concat_axis=1, tiled=True)


def to_blocks(values):
    return lax.all_to_all(values, "tensor", split_axis=1, concat_axis=0, tiled=True)


def make(n_dp):
    def on_device(tokens_in, right_one, left_one, right_two, left_two, out_grad):
        bf = jnp.bfloat16
        f32 = jnp.float32

        def dot(spec, a, b):
            return jnp.einsum(spec, a, b, preferred_element_type=f32)

        u1 = dot("tbi,bio->tbo", tokens_in, right_one).astype(bf)
        v1 = to_tokens(u1)
        left_one = gather_factor(left_one, n_dp)
        right_two = gather_factor(right_two, n_dp)
        left_two = gather_factor(left_two, n_dp)
        dw_two = to_tokens(out_grad)
        z1 = dot("tbj,jbk->tjk", v1, left_one).astype(bf)
        hidden = gelu_value(z1.astype(f32)).astype(bf)
        u2 = dot("tjk,kjm->tkm", hidden, right_two).astype(bf)
        w2 = dot("tkm,mkn->tnm", u2, left_two).astype(bf)
        mixed = to_blocks(w2)
        layer_out = (tokens_in.astype(f32) + mixed.astype(f32)).astype(bf)
        du2 = dot("tnm,mkn->tkm", dw_two, left_two).astype(bf)
        gl2 = reduce_all(dot("tkm,tnm->mkn", u2, dw_two))
        gr2 = reduce_all(dot("tjk,tkm->kjm", hidden, du2))
        dh = dot("tkm,kjm->tjk", du2, right_two)
        dz1 = (dh * gelu_slope(z1.astype(f32))).astype(bf)
        dv1 = dot("tjk,jbk->tbj", dz1, left_one).astype(bf)
        du1 = to_blocks(dv1)
        gl1 = reduce_all(dot("tbj,tjk->jbk", v1, dz1))
        gr1 = dot("tbi,tbo->bio", tokens_in, du1)
        input_grad = (out_grad.astype(f32) + dot("tbo,bio->tbi", du1, right_one)).astype(bf)
        gr1 = lax.psum_scatter(gr1, "dp", scatter_dimension=1, tiled=True)
        return (layer_out, input_grad, gr1, gl1, gr2, gl2)

    return on_device


def solution(mesh):
    split = P("dp", "tensor", None)
    factor = P("tensor", None, None)
    grad = P("tensor", "dp", None)
    return jax.shard_map(
        make(mesh.shape["dp"]),
        mesh=mesh,
        in_specs=(split, factor, factor, factor, factor, split),
        out_specs=(split, split, grad, grad, grad, grad),
        check_vma=False,
    )
```

```python
import math

import jax
import jax.numpy as jnp
from jax import lax
from jax.experimental import pallas as pl
from jax.experimental.pallas import tpu as pltpu
from jax.sharding import PartitionSpec as P


def gelu_value(z):
    return 0.5 * z * (1.0 + lax.erf(z / math.sqrt(2.0)))


def gelu_slope(z):
    return 0.5 * (1.0 + lax.erf(z / math.sqrt(2.0))) + z * jnp.exp(-0.5 * z * z) / math.sqrt(
        2.0 * math.pi
    )


MESH = pl.DeviceIdType.MESH


def place():
    rank = lax.axis_index("tensor")
    return lax.axis_index("dp"), lax.div(rank, 2), lax.rem(rank, 2)


def greet(peers):
    barrier = pltpu.get_barrier_semaphore()
    for peer in peers:
        pl.semaphore_signal(barrier, inc=1, device_id=peer, device_id_type=MESH)
    pl.semaphore_wait(barrier, len(peers))


def peers_of(n_dp, n_z):
    d, z, c = place()
    along_z = [(d, lax.rem(z + k, n_z) * 2 + c) for k in range(1, n_z)]
    along_dp = [(lax.rem(d + k, n_dp), z * 2 + c) for k in range(1, n_dp)]
    return along_z, along_dp, (d, z * 2 + 1 - c)


def remote(src, dst, send, recv, peer):
    return pltpu.make_async_remote_copy(
        src_ref=src, dst_ref=dst, send_sem=send, recv_sem=recv, device_id=peer, device_id_type=MESH
    )


def gather_kernel(n_dp, n_z, count, *refs):
    shards, (sent, wholes), sems = refs[:count], (refs[count], refs[count + 1 : 2 * count + 1]), refs[2 * count + 1 :]
    got = sems[0]
    own_sem, zs, zr, ds, dr, cs, cr, us, ur, ul = sems[1:]
    d, z, c = place()
    n = n_z * 2
    rank = z * 2 + c
    along_z, along_dp, sibling = peers_of(n_dp, n_z)
    others = [lax.rem(rank + k, n) for k in range(1, n)]
    greet([(d, p) for p in others] + along_dp)
    swaps = [remote(sent.at[p], got.at[rank], us.at[i], ur.at[i], (d, p)) for i, p in enumerate(others)]
    keep = pltpu.make_async_copy(sent.at[rank], got.at[rank], ul)
    stage_z, own = [], []
    for f in range(count):
        own.append(pltpu.make_async_copy(shards[f].at[d], wholes[f].at[z, c, d], own_sem.at[f]))
        stage_z.append([
            remote(shards[f].at[d], wholes[f].at[z, c, d], zs.at[f, i], zr.at[f, i], p)
            for i, p in enumerate(along_z)
        ])
    for f in range(count):
        own[f].start()
        for copy in stage_z[f]:
            copy.start()
    stage_dp = []
    for f in range(count):
        own[f].wait()
        for copy in stage_z[f]:
            copy.wait()
        part = wholes[f].at[:, c, d]
        stage_dp.append([remote(part, part, ds.at[f, i], dr.at[f, i], p) for i, p in enumerate(along_dp)])
        for copy in stage_dp[f]:
            copy.start()
    keep.start()
    for copy in swaps:
        copy.start()
    stage_core = []
    for f in range(count):
        for copy in stage_dp[f]:
            copy.wait()
        half = wholes[f].at[:, c]
        stage_core.append(remote(half, half, cs.at[f], cr.at[f], sibling))
        stage_core[f].start()
    for copy in stage_core:
        copy.wait()
    keep.wait()
    for copy in swaps:
        copy.wait()


def gather_and_swap(values, factors, n_dp, n_z):
    count, n = len(factors), n_z * 2
    blocks, rows, cols = factors[0].shape
    part = blocks * rows // n_dp
    shards = [f.reshape(n_dp, part, cols) for f in factors]
    sent = values.reshape((n, values.shape[0] // n) + values.shape[1:])
    dma = pltpu.SemaphoreType.DMA
    hbm = pl.BlockSpec(memory_space=pl.ANY)
    out = pl.pallas_call(
        lambda *refs: gather_kernel(n_dp, n_z, count, *refs),
        out_shape=[jax.ShapeDtypeStruct((n_z, 2, n_dp, part, cols), f.dtype) for f in factors]
        + [jax.ShapeDtypeStruct(sent.shape, sent.dtype)],
        in_specs=[hbm] * (count + 1),
        out_specs=[hbm] * (count + 1),
        scratch_shapes=[
            dma((count,)),
            dma((count, n_z - 1)),
            dma((count, n_z - 1)),
            dma((count, n_dp - 1)),
            dma((count, n_dp - 1)),
            dma((count,)),
            dma((count,)),
            dma((n - 1,)),
            dma((n - 1,)),
            dma,
        ],
        compiler_params=pltpu.CompilerParams(collective_id=0, has_side_effects=True),
        cost_estimate=pl.CostEstimate(flops=0, bytes_accessed=64 * 2**20, transcendentals=0),
    )(*shards, sent)
    return [w.reshape(n * blocks, rows, cols) for w in out[:count]], out[count]


def reduce_kernel(n_dp, n_z, count, *refs):
    f32, bf = jnp.float32, jnp.bfloat16
    grads, outs, rest = refs[:count], refs[count : 2 * count], refs[2 * count :]
    own, got_c, sum_c, got_d, sum_d, got_z, own_sem, cs, cr, ds, dr, zs, zr = rest
    d, z, c = place()
    along_z, along_dp, sibling = peers_of(n_dp, n_z)
    greet(along_z + along_dp + [sibling])
    stage_c, local = [], []
    for f in range(count):
        stage_c.append(remote(grads[f].at[:, 1 - c], got_c.at[f], cs.at[f], cr.at[f], sibling))
        local.append(pltpu.make_async_copy(grads[f].at[:, c], own.at[f], own_sem.at[f]))
        stage_c[f].start()
        local[f].start()
    stage_d = []
    for f in range(count):
        stage_c[f].wait()
        local[f].wait()

        def core_sum(k, carry):
            for q in range(n_dp):
                total = own[f, k, :, q].astype(f32) + got_c[f, k, :, q].astype(f32)
                sum_c[f, q, k] = total.astype(bf)
            return carry

        lax.fori_loop(0, n_z, core_sum, 0)
        stage_d.append([
            remote(sum_c.at[f, p[0]], got_d.at[f, i], ds.at[f, i], dr.at[f, i], p)
            for i, p in enumerate(along_dp)
        ])
        for copy in stage_d[f]:
            copy.start()
    stage_z = []
    for f in range(count):
        for copy in stage_d[f]:
            copy.wait()

        def dp_sum(k, carry):
            total = sum_c[f, d, k].astype(f32)
            for i in range(n_dp - 1):
                total += got_d[f, i, k].astype(f32)
            sum_d[f, k] = total.astype(bf)
            return carry

        lax.fori_loop(0, n_z, dp_sum, 0)
        stage_z.append([
            remote(sum_d.at[f, lax.rem(z + i + 1, n_z)], got_z.at[f, i], zs.at[f, i], zr.at[f, i], p)
            for i, p in enumerate(along_z)
        ])
        for copy in stage_z[f]:
            copy.start()
    for f in range(count):
        for copy in stage_z[f]:
            copy.wait()
        total = sum_d[f, z].astype(f32)
        for i in range(n_z - 1):
            total += got_z[f, i].astype(f32)
        outs[f][...] = total


def reduce_all(grads, n_dp, n_z):
    count = len(grads)
    blocks, rows, cols = grads[0].shape
    own, strip = blocks // (2 * n_z), rows // n_dp
    bf = jnp.bfloat16
    parts = [g.astype(bf).reshape(n_z, 2, own, n_dp, strip, cols) for g in grads]
    dma = pltpu.SemaphoreType.DMA
    piece = (own, strip, cols)
    return pl.pallas_call(
        lambda *refs: reduce_kernel(n_dp, n_z, count, *refs),
        out_shape=[jax.ShapeDtypeStruct(piece, jnp.float32)] * count,
        in_specs=[pl.BlockSpec(memory_space=pl.ANY)] * count,
        out_specs=[pl.BlockSpec(memory_space=pltpu.VMEM)] * count,
        scratch_shapes=[
            pltpu.VMEM((count, n_z, own, n_dp, strip, cols), bf),
            pltpu.VMEM((count, n_z, own, n_dp, strip, cols), bf),
            pltpu.VMEM((count, n_dp, n_z) + piece, bf),
            pltpu.VMEM((count, n_dp - 1, n_z) + piece, bf),
            pltpu.VMEM((count, n_z) + piece, bf),
            pltpu.VMEM((count, n_z - 1) + piece, bf),
            dma((count,)),
            dma((count,)),
            dma((count,)),
            dma((count, n_dp - 1)),
            dma((count, n_dp - 1)),
            dma((count, n_z - 1)),
            dma((count, n_z - 1)),
        ],
        compiler_params=pltpu.CompilerParams(
            collective_id=1, has_side_effects=True, vmem_limit_bytes=40 * 2**20
        ),
        cost_estimate=pl.CostEstimate(flops=0, bytes_accessed=64 * 2**20, transcendentals=0),
    )(*parts)


def to_tokens(values):
    return lax.all_to_all(values, "tensor", split_axis=0, concat_axis=1, tiled=True)


def to_blocks(values):
    return lax.all_to_all(values, "tensor", split_axis=1, concat_axis=0, tiled=True)


def make(n_dp, n_z):
    def on_device(tokens_in, right_one, left_one, right_two, left_two, out_grad):
        bf = jnp.bfloat16
        f32 = jnp.float32

        def dot(spec, a, b):
            return jnp.einsum(spec, a, b, preferred_element_type=f32)

        u1 = dot("tbi,bio->tbo", tokens_in, right_one).astype(bf)
        (left_one, right_two, left_two), v1 = gather_and_swap(
            u1, (left_one, right_two, left_two), n_dp, n_z
        )
        v1 = jnp.swapaxes(v1, 0, 1).reshape(v1.shape[1], -1, v1.shape[3])
        v1, late_grad = lax.optimization_barrier((v1, out_grad))
        dw_two = to_tokens(late_grad)
        z1 = dot("tbj,jbk->tjk", v1, left_one).astype(bf)
        hidden = gelu_value(z1.astype(f32)).astype(bf)
        u2 = dot("tjk,kjm->tkm", hidden, right_two).astype(bf)
        w2 = dot("tkm,mkn->tnm", u2, left_two).astype(bf)
        mixed = to_blocks(w2)
        layer_out = (tokens_in.astype(f32) + mixed.astype(f32)).astype(bf)
        du2 = dot("tnm,mkn->tkm", dw_two, left_two).astype(bf)
        gl2 = dot("tkm,tnm->mkn", u2, dw_two)
        gr2 = dot("tjk,tkm->kjm", hidden, du2)
        dh = dot("tkm,kjm->tjk", du2, right_two)
        dz1 = (dh * gelu_slope(z1.astype(f32))).astype(bf)
        dv1 = dot("tjk,jbk->tbj", dz1, left_one).astype(bf)
        du1 = to_blocks(dv1)
        gl1 = dot("tbj,tjk->jbk", v1, dz1)
        gl2, gr2, gl1 = reduce_all((gl2, gr2, gl1), n_dp, n_z)
        gr1 = dot("tbi,tbo->bio", tokens_in, du1)
        input_grad = (out_grad.astype(f32) + dot("tbo,bio->tbi", du1, right_one)).astype(bf)
        gr1 = gr1.astype(bf).reshape(gr1.shape[0], n_dp, -1, gr1.shape[2])
        gr1 = lax.all_to_all(gr1, "dp", split_axis=1, concat_axis=1, tiled=True)
        gr1 = jnp.sum(gr1.astype(f32), axis=1)
        return (layer_out, input_grad, gr1, gl1, gr2, gl2)

    return on_device


def solution(mesh):
    split = P("dp", "tensor", None)
    factor = P("tensor", None, None)
    grad = P("tensor", "dp", None)
    return jax.shard_map(
        make(mesh.shape["dp"], mesh.shape["tensor"] // 2),
        mesh=mesh,
        in_specs=(split, factor, factor, factor, factor, split),
        out_specs=(split, split, grad, grad, grad, grad),
        check_vma=False,
    )
```

```python
import math

import jax
import jax.numpy as jnp
from jax import lax
from jax.experimental import pallas as pl
from jax.experimental.pallas import tpu as pltpu
from jax.sharding import PartitionSpec as P


def gelu_value(z):
    return 0.5 * z * (1.0 + lax.erf(z / math.sqrt(2.0)))


def gelu_slope(z):
    return 0.5 * (1.0 + lax.erf(z / math.sqrt(2.0))) + z * jnp.exp(-0.5 * z * z) / math.sqrt(
        2.0 * math.pi
    )


MESH = pl.DeviceIdType.MESH


def place():
    rank = lax.axis_index("tensor")
    return lax.axis_index("dp"), lax.div(rank, 2), lax.rem(rank, 2)


def greet(peers):
    barrier = pltpu.get_barrier_semaphore()
    for peer in peers:
        pl.semaphore_signal(barrier, inc=1, device_id=peer, device_id_type=MESH)
    pl.semaphore_wait(barrier, len(peers))


def peers_of(n_dp, n_z):
    d, z, c = place()
    along_z = [(d, lax.rem(z + k, n_z) * 2 + c) for k in range(1, n_z)]
    along_dp = [(lax.rem(d + k, n_dp), z * 2 + c) for k in range(1, n_dp)]
    return along_z, along_dp, (d, z * 2 + 1 - c)


def remote(src, dst, send, recv, peer):
    return pltpu.make_async_remote_copy(
        src_ref=src, dst_ref=dst, send_sem=send, recv_sem=recv, device_id=peer, device_id_type=MESH
    )


def halves_of(n_dp):
    return 2, n_dp // 2


def gather_kernel(n_dp, n_z, count, *refs):
    shards, (sent, wholes), sems = refs[:count], (refs[count], refs[count + 1 : 2 * count + 1]), refs[2 * count + 1 :]
    got = sems[0]
    own_sem, zs, zr, ls, lr, hs, hr, cs, cr, us, ur, ul = sems[1:]
    n_hi, n_lo = halves_of(n_dp)
    d, z, c = place()
    n = n_z * 2
    rank = z * 2 + c
    along_z, along_dp, sibling = peers_of(n_dp, n_z)
    others = [lax.rem(rank + k, n) for k in range(1, n)]
    hi, lo = lax.div(d, n_lo), lax.rem(d, n_lo)
    along_lo = [(hi * n_lo + lax.rem(lo + k, n_lo), rank) for k in range(1, n_lo)]
    along_hi = [(lax.rem(hi + k, n_hi) * n_lo + lo, rank) for k in range(1, n_hi)]
    greet([(d, p) for p in others] + along_lo + along_hi)
    swaps = [remote(sent.at[p], got.at[rank], us.at[i], ur.at[i], (d, p)) for i, p in enumerate(others)]
    keep = pltpu.make_async_copy(sent.at[rank], got.at[rank], ul)
    stage_z, own = [], []
    for f in range(count):
        own.append(pltpu.make_async_copy(shards[f].at[d], wholes[f].at[z, c, hi, lo], own_sem.at[f]))
        stage_z.append([
            remote(shards[f].at[d], wholes[f].at[z, c, hi, lo], zs.at[f, i], zr.at[f, i], p)
            for i, p in enumerate(along_z)
        ])
    for f in range(count):
        own[f].start()
        for copy in stage_z[f]:
            copy.start()

    def spread(f, stage, lo_part, hi_part):
        copies = [
            remote(lo_part, lo_part, ls.at[f, stage, i], lr.at[f, stage, i], p) for i, p in enumerate(along_lo)
        ] + [
            remote(hi_part, hi_part, hs.at[f, stage, i], hr.at[f, stage, i], p) for i, p in enumerate(along_hi)
        ]
        for copy in copies:
            copy.start()
        return copies

    first = []
    for f in range(count):
        own[f].wait()
        for copy in stage_z[f]:
            copy.wait()
        first.append(spread(f, 0, wholes[f].at[:, c, hi, lo, 0], wholes[f].at[:, c, hi, lo, 1]))
    keep.start()
    for copy in swaps:
        copy.start()
    second = []
    for f in range(count):
        for copy in first[f]:
            copy.wait()
        second.append(spread(f, 1, wholes[f].at[:, c, :, lo, 1], wholes[f].at[:, c, hi, :, 0]))
    stage_core = []
    for f in range(count):
        for copy in second[f]:
            copy.wait()
        half = wholes[f].at[:, c]
        stage_core.append(remote(half, half, cs.at[f], cr.at[f], sibling))
        stage_core[f].start()
    for copy in stage_core:
        copy.wait()
    keep.wait()
    for copy in swaps:
        copy.wait()


def gather_and_swap(values, factors, n_dp, n_z):
    count, n = len(factors), n_z * 2
    blocks, rows, cols = factors[0].shape
    part = blocks * rows // n_dp
    n_hi, n_lo = halves_of(n_dp)
    shards = [f.reshape(n_dp, 2, part // 2, cols) for f in factors]
    sent = values.reshape((n, values.shape[0] // n) + values.shape[1:])
    dma = pltpu.SemaphoreType.DMA
    hbm = pl.BlockSpec(memory_space=pl.ANY)
    out = pl.pallas_call(
        lambda *refs: gather_kernel(n_dp, n_z, count, *refs),
        out_shape=[jax.ShapeDtypeStruct((n_z, 2, n_hi, n_lo, 2, part // 2, cols), f.dtype) for f in factors]
        + [jax.ShapeDtypeStruct(sent.shape, sent.dtype)],
        in_specs=[hbm] * (count + 1),
        out_specs=[hbm] * (count + 1),
        scratch_shapes=[
            dma((count,)),
            dma((count, n_z - 1)),
            dma((count, n_z - 1)),
            dma((count, 2, n_lo - 1)),
            dma((count, 2, n_lo - 1)),
            dma((count, 2, n_hi - 1)),
            dma((count, 2, n_hi - 1)),
            dma((count,)),
            dma((count,)),
            dma((n - 1,)),
            dma((n - 1,)),
            dma,
        ],
        compiler_params=pltpu.CompilerParams(collective_id=0, has_side_effects=True),
        cost_estimate=pl.CostEstimate(flops=0, bytes_accessed=64 * 2**20, transcendentals=0),
    )(*shards, sent)
    return [w.reshape(n * blocks, rows, cols) for w in out[:count]], out[count]


def reduce_kernel(n_dp, n_z, count, *refs):
    f32, bf = jnp.float32, jnp.bfloat16
    grads, outs, rest = refs[:count], refs[count : 2 * count], refs[2 * count :]
    own, got_c, sum_c, got_d, sum_d, got_z, own_sem, cs, cr, ds, dr, zs, zr = rest
    d, z, c = place()
    along_z, along_dp, sibling = peers_of(n_dp, n_z)
    greet(along_z + along_dp + [sibling])
    stage_c, local = [], []
    for f in range(count):
        stage_c.append(remote(grads[f].at[:, 1 - c], got_c.at[f], cs.at[f], cr.at[f], sibling))
        local.append(pltpu.make_async_copy(grads[f].at[:, c], own.at[f], own_sem.at[f]))
        stage_c[f].start()
        local[f].start()
    stage_d = []
    for f in range(count):
        stage_c[f].wait()
        local[f].wait()

        def core_sum(k, carry):
            for q in range(n_dp):
                total = own[f, k, :, q].astype(f32) + got_c[f, k, :, q].astype(f32)
                sum_c[f, q, k] = total.astype(bf)
            return carry

        lax.fori_loop(0, n_z, core_sum, 0)
        stage_d.append([
            remote(sum_c.at[f, p[0]], got_d.at[f, i], ds.at[f, i], dr.at[f, i], p)
            for i, p in enumerate(along_dp)
        ])
        for copy in stage_d[f]:
            copy.start()
    stage_z = []
    for f in range(count):
        for copy in stage_d[f]:
            copy.wait()

        def dp_sum(k, carry):
            total = sum_c[f, d, k].astype(f32)
            for i in range(n_dp - 1):
                total += got_d[f, i, k].astype(f32)
            sum_d[f, k] = total.astype(bf)
            return carry

        lax.fori_loop(0, n_z, dp_sum, 0)
        stage_z.append([
            remote(sum_d.at[f, lax.rem(z + i + 1, n_z)], got_z.at[f, i], zs.at[f, i], zr.at[f, i], p)
            for i, p in enumerate(along_z)
        ])
        for copy in stage_z[f]:
            copy.start()
    for f in range(count):
        for copy in stage_z[f]:
            copy.wait()
        total = sum_d[f, z].astype(f32)
        for i in range(n_z - 1):
            total += got_z[f, i].astype(f32)
        outs[f][...] = total


def reduce_all(grads, n_dp, n_z):
    count = len(grads)
    blocks, rows, cols = grads[0].shape
    own, strip = blocks // (2 * n_z), rows // n_dp
    bf = jnp.bfloat16
    parts = [g.astype(bf).reshape(n_z, 2, own, n_dp, strip, cols) for g in grads]
    dma = pltpu.SemaphoreType.DMA
    piece = (own, strip, cols)
    return pl.pallas_call(
        lambda *refs: reduce_kernel(n_dp, n_z, count, *refs),
        out_shape=[jax.ShapeDtypeStruct(piece, jnp.float32)] * count,
        in_specs=[pl.BlockSpec(memory_space=pl.ANY)] * count,
        out_specs=[pl.BlockSpec(memory_space=pltpu.VMEM)] * count,
        scratch_shapes=[
            pltpu.VMEM((count, n_z, own, n_dp, strip, cols), bf),
            pltpu.VMEM((count, n_z, own, n_dp, strip, cols), bf),
            pltpu.VMEM((count, n_dp, n_z) + piece, bf),
            pltpu.VMEM((count, n_dp - 1, n_z) + piece, bf),
            pltpu.VMEM((count, n_z) + piece, bf),
            pltpu.VMEM((count, n_z - 1) + piece, bf),
            dma((count,)),
            dma((count,)),
            dma((count,)),
            dma((count, n_dp - 1)),
            dma((count, n_dp - 1)),
            dma((count, n_z - 1)),
            dma((count, n_z - 1)),
        ],
        compiler_params=pltpu.CompilerParams(
            collective_id=1, has_side_effects=True, vmem_limit_bytes=40 * 2**20
        ),
        cost_estimate=pl.CostEstimate(flops=0, bytes_accessed=64 * 2**20, transcendentals=0),
    )(*parts)


def to_tokens(values):
    return lax.all_to_all(values, "tensor", split_axis=0, concat_axis=1, tiled=True)


def to_blocks(values):
    return lax.all_to_all(values, "tensor", split_axis=1, concat_axis=0, tiled=True)


def make(n_dp, n_z):
    def on_device(tokens_in, right_one, left_one, right_two, left_two, out_grad):
        bf = jnp.bfloat16
        f32 = jnp.float32

        def dot(spec, a, b):
            return jnp.einsum(spec, a, b, preferred_element_type=f32)

        u1 = dot("tbi,bio->tbo", tokens_in, right_one).astype(bf)
        (left_one, right_two, left_two), v1 = gather_and_swap(
            u1, (left_one, right_two, left_two), n_dp, n_z
        )
        v1 = jnp.swapaxes(v1, 0, 1).reshape(v1.shape[1], -1, v1.shape[3])
        v1, late_grad = lax.optimization_barrier((v1, out_grad))
        dw_two = to_tokens(late_grad)
        z1 = dot("tbj,jbk->tjk", v1, left_one).astype(bf)
        hidden = gelu_value(z1.astype(f32)).astype(bf)
        u2 = dot("tjk,kjm->tkm", hidden, right_two).astype(bf)
        w2 = dot("tkm,mkn->tnm", u2, left_two).astype(bf)
        dw_two, w2 = lax.optimization_barrier((dw_two, w2))
        mixed = to_blocks(w2)
        layer_out = (tokens_in.astype(f32) + mixed.astype(f32)).astype(bf)
        du2 = dot("tnm,mkn->tkm", dw_two, left_two).astype(bf)
        gl2 = dot("tkm,tnm->mkn", u2, dw_two)
        gr2 = dot("tjk,tkm->kjm", hidden, du2)
        dh = dot("tkm,kjm->tjk", du2, right_two)
        dz1 = (dh * gelu_slope(z1.astype(f32))).astype(bf)
        dv1 = dot("tjk,jbk->tbj", dz1, left_one).astype(bf)
        gl1 = dot("tbj,tjk->jbk", v1, dz1)
        dv1, gl2, gr2, gl1 = lax.optimization_barrier((dv1, gl2.astype(bf), gr2.astype(bf), gl1.astype(bf)))
        du1 = to_blocks(dv1)
        gl2, gr2, gl1 = reduce_all((gl2, gr2, gl1), n_dp, n_z)
        gr1 = dot("tbi,tbo->bio", tokens_in, du1)
        input_grad = (out_grad.astype(f32) + dot("tbo,bio->tbi", du1, right_one)).astype(bf)
        gr1 = gr1.astype(bf).reshape(gr1.shape[0], n_dp, -1, gr1.shape[2])
        gr1 = lax.all_to_all(gr1, "dp", split_axis=1, concat_axis=1, tiled=True)
        gr1 = jnp.sum(gr1.astype(f32), axis=1)
        return (layer_out, input_grad, gr1, gl1, gr2, gl2)

    return on_device


def solution(mesh):
    split = P("dp", "tensor", None)
    factor = P("tensor", None, None)
    grad = P("tensor", "dp", None)
    return jax.shard_map(
        make(mesh.shape["dp"], mesh.shape["tensor"] // 2),
        mesh=mesh,
        in_specs=(split, factor, factor, factor, factor, split),
        out_specs=(split, split, grad, grad, grad, grad),
        check_vma=False,
    )
```

```python
import math

import jax
import jax.numpy as jnp
from jax import lax
from jax.experimental import pallas as pl
from jax.experimental.pallas import tpu as pltpu
from jax.sharding import PartitionSpec as P


def gelu_value(z):
    return 0.5 * z * (1.0 + lax.erf(z / math.sqrt(2.0)))


def gelu_slope(z):
    return 0.5 * (1.0 + lax.erf(z / math.sqrt(2.0))) + z * jnp.exp(-0.5 * z * z) / math.sqrt(
        2.0 * math.pi
    )


MESH = pl.DeviceIdType.MESH


def place():
    rank = lax.axis_index("tensor")
    return lax.axis_index("dp"), lax.div(rank, 2), lax.rem(rank, 2)


def greet(peers):
    barrier = pltpu.get_barrier_semaphore()
    for peer in peers:
        pl.semaphore_signal(barrier, inc=1, device_id=peer, device_id_type=MESH)
    pl.semaphore_wait(barrier, len(peers))


def peers_of(n_dp, n_z):
    d, z, c = place()
    along_z = [(d, lax.rem(z + k, n_z) * 2 + c) for k in range(1, n_z)]
    along_dp = [(lax.rem(d + k, n_dp), z * 2 + c) for k in range(1, n_dp)]
    return along_z, along_dp, (d, z * 2 + 1 - c)


def remote(src, dst, send, recv, peer):
    return pltpu.make_async_remote_copy(
        src_ref=src, dst_ref=dst, send_sem=send, recv_sem=recv, device_id=peer, device_id_type=MESH
    )


def halves_of(n_dp):
    return 2, n_dp // 2


def gather_kernel(n_dp, n_z, count, *refs):
    shards, (sent, wholes), sems = refs[:count], (refs[count], refs[count + 1 : 2 * count + 1]), refs[2 * count + 1 :]
    got = sems[0]
    own_sem, zs, zr, ls, lr, hs, hr, cs, cr, us, ur, ul = sems[1:]
    n_hi, n_lo = halves_of(n_dp)
    d, z, c = place()
    n = n_z * 2
    rank = z * 2 + c
    along_z, along_dp, sibling = peers_of(n_dp, n_z)
    others = [lax.rem(rank + k, n) for k in range(1, n)]
    hi, lo = lax.div(d, n_lo), lax.rem(d, n_lo)
    along_lo = [(hi * n_lo + lax.rem(lo + k, n_lo), rank) for k in range(1, n_lo)]
    along_hi = [(lax.rem(hi + k, n_hi) * n_lo + lo, rank) for k in range(1, n_hi)]
    greet([(d, p) for p in others] + along_lo + along_hi)
    swaps = [remote(sent.at[p], got.at[rank], us.at[i], ur.at[i], (d, p)) for i, p in enumerate(others)]
    keep = pltpu.make_async_copy(sent.at[rank], got.at[rank], ul)
    stage_z, own = [], []
    for f in range(count):
        own.append(pltpu.make_async_copy(shards[f].at[d], wholes[f].at[z, c, hi, lo], own_sem.at[f]))
        stage_z.append([
            remote(shards[f].at[d], wholes[f].at[z, c, hi, lo], zs.at[f, i], zr.at[f, i], p)
            for i, p in enumerate(along_z)
        ])
    for f in range(count):
        own[f].start()
    for copy in stage_z[0]:
        copy.start()

    def spread(f, stage, lo_part, hi_part):
        copies = [
            remote(lo_part, lo_part, ls.at[f, stage, i], lr.at[f, stage, i], p) for i, p in enumerate(along_lo)
        ] + [
            remote(hi_part, hi_part, hs.at[f, stage, i], hr.at[f, stage, i], p) for i, p in enumerate(along_hi)
        ]
        for copy in copies:
            copy.start()
        return copies

    first = []
    for f in range(count):
        own[f].wait()
        for copy in stage_z[f]:
            copy.wait()
        if f + 1 < count:
            for copy in stage_z[f + 1]:
                copy.start()
        first.append(spread(f, 0, wholes[f].at[:, c, hi, lo, 0], wholes[f].at[:, c, hi, lo, 1]))
    keep.start()
    for copy in swaps:
        copy.start()
    second = []
    for f in range(count):
        for copy in first[f]:
            copy.wait()
        second.append(spread(f, 1, wholes[f].at[:, c, :, lo, 1], wholes[f].at[:, c, hi, :, 0]))
    stage_core = []
    for f in range(count):
        for copy in second[f]:
            copy.wait()
        half = wholes[f].at[:, c]
        stage_core.append(remote(half, half, cs.at[f], cr.at[f], sibling))
        stage_core[f].start()
    for copy in stage_core:
        copy.wait()
    keep.wait()
    for copy in swaps:
        copy.wait()


def gather_and_swap(values, factors, n_dp, n_z):
    count, n = len(factors), n_z * 2
    blocks, rows, cols = factors[0].shape
    part = blocks * rows // n_dp
    n_hi, n_lo = halves_of(n_dp)
    shards = [f.reshape(n_dp, 2, part // 2, cols) for f in factors]
    sent = values.reshape((n, values.shape[0] // n) + values.shape[1:])
    dma = pltpu.SemaphoreType.DMA
    hbm = pl.BlockSpec(memory_space=pl.ANY)
    out = pl.pallas_call(
        lambda *refs: gather_kernel(n_dp, n_z, count, *refs),
        out_shape=[jax.ShapeDtypeStruct((n_z, 2, n_hi, n_lo, 2, part // 2, cols), f.dtype) for f in factors]
        + [jax.ShapeDtypeStruct(sent.shape, sent.dtype)],
        in_specs=[hbm] * (count + 1),
        out_specs=[hbm] * (count + 1),
        scratch_shapes=[
            dma((count,)),
            dma((count, n_z - 1)),
            dma((count, n_z - 1)),
            dma((count, 2, n_lo - 1)),
            dma((count, 2, n_lo - 1)),
            dma((count, 2, n_hi - 1)),
            dma((count, 2, n_hi - 1)),
            dma((count,)),
            dma((count,)),
            dma((n - 1,)),
            dma((n - 1,)),
            dma,
        ],
        compiler_params=pltpu.CompilerParams(collective_id=0, has_side_effects=True),
        cost_estimate=pl.CostEstimate(flops=0, bytes_accessed=64 * 2**20, transcendentals=0),
    )(*shards, sent)
    return [w.reshape(n * blocks, rows, cols) for w in out[:count]], out[count]


def reduce_kernel(n_dp, n_z, count, *refs):
    f32, bf = jnp.float32, jnp.bfloat16
    grads, outs, rest = refs[:count], refs[count : 2 * count], refs[2 * count :]
    own, got_c, sum_c, got_d, sum_d, got_z, own_sem, cs, cr, ds, dr, zs, zr = rest
    d, z, c = place()
    along_z, along_dp, sibling = peers_of(n_dp, n_z)
    greet(along_z + along_dp + [sibling])
    stage_c, local = [], []
    for f in range(count):
        stage_c.append(remote(grads[f].at[:, 1 - c], got_c.at[f], cs.at[f], cr.at[f], sibling))
        local.append(pltpu.make_async_copy(grads[f].at[:, c], own.at[f], own_sem.at[f]))
        local[f].start()
    stage_c[0].start()
    stage_d = []
    for f in range(count):
        stage_c[f].wait()
        local[f].wait()
        if f + 1 < count:
            stage_c[f + 1].start()

        def core_sum(k, carry):
            for q in range(n_dp):
                total = own[f, k, :, q].astype(f32) + got_c[f, k, :, q].astype(f32)
                sum_c[f, q, k] = total.astype(bf)
            return carry

        lax.fori_loop(0, n_z, core_sum, 0)
        stage_d.append([
            remote(sum_c.at[f, p[0]], got_d.at[f, i], ds.at[f, i], dr.at[f, i], p)
            for i, p in enumerate(along_dp)
        ])
        for copy in stage_d[f]:
            copy.start()
    stage_z = []
    for f in range(count):
        for copy in stage_d[f]:
            copy.wait()

        def dp_sum(k, carry):
            total = sum_c[f, d, k].astype(f32)
            for i in range(n_dp - 1):
                total += got_d[f, i, k].astype(f32)
            sum_d[f, k] = total.astype(bf)
            return carry

        lax.fori_loop(0, n_z, dp_sum, 0)
        stage_z.append([
            remote(sum_d.at[f, lax.rem(z + i + 1, n_z)], got_z.at[f, i], zs.at[f, i], zr.at[f, i], p)
            for i, p in enumerate(along_z)
        ])
        for copy in stage_z[f]:
            copy.start()
    for f in range(count):
        for copy in stage_z[f]:
            copy.wait()
        total = sum_d[f, z].astype(f32)
        for i in range(n_z - 1):
            total += got_z[f, i].astype(f32)
        outs[f][...] = total


def reduce_all(grads, n_dp, n_z):
    count = len(grads)
    blocks, rows, cols = grads[0].shape
    own, strip = blocks // (2 * n_z), rows // n_dp
    bf = jnp.bfloat16
    parts = [g.astype(bf).reshape(n_z, 2, own, n_dp, strip, cols) for g in grads]
    dma = pltpu.SemaphoreType.DMA
    piece = (own, strip, cols)
    return pl.pallas_call(
        lambda *refs: reduce_kernel(n_dp, n_z, count, *refs),
        out_shape=[jax.ShapeDtypeStruct(piece, jnp.float32)] * count,
        in_specs=[pl.BlockSpec(memory_space=pl.ANY)] * count,
        out_specs=[pl.BlockSpec(memory_space=pltpu.VMEM)] * count,
        scratch_shapes=[
            pltpu.VMEM((count, n_z, own, n_dp, strip, cols), bf),
            pltpu.VMEM((count, n_z, own, n_dp, strip, cols), bf),
            pltpu.VMEM((count, n_dp, n_z) + piece, bf),
            pltpu.VMEM((count, n_dp - 1, n_z) + piece, bf),
            pltpu.VMEM((count, n_z) + piece, bf),
            pltpu.VMEM((count, n_z - 1) + piece, bf),
            dma((count,)),
            dma((count,)),
            dma((count,)),
            dma((count, n_dp - 1)),
            dma((count, n_dp - 1)),
            dma((count, n_z - 1)),
            dma((count, n_z - 1)),
        ],
        compiler_params=pltpu.CompilerParams(
            collective_id=1, has_side_effects=True, vmem_limit_bytes=40 * 2**20
        ),
        cost_estimate=pl.CostEstimate(flops=0, bytes_accessed=64 * 2**20, transcendentals=0),
    )(*parts)


def to_tokens(values):
    return lax.all_to_all(values, "tensor", split_axis=0, concat_axis=1, tiled=True)


def to_blocks(values):
    return lax.all_to_all(values, "tensor", split_axis=1, concat_axis=0, tiled=True)


def make(n_dp, n_z):
    def on_device(tokens_in, right_one, left_one, right_two, left_two, out_grad):
        bf = jnp.bfloat16
        f32 = jnp.float32

        def dot(spec, a, b):
            return jnp.einsum(spec, a, b, preferred_element_type=f32)

        u1 = dot("tbi,bio->tbo", tokens_in, right_one).astype(bf)
        (left_one, right_two, left_two), v1 = gather_and_swap(
            u1, (left_one, right_two, left_two), n_dp, n_z
        )
        v1 = jnp.swapaxes(v1, 0, 1).reshape(v1.shape[1], -1, v1.shape[3])
        v1, late_grad = lax.optimization_barrier((v1, out_grad))
        dw_two = to_tokens(late_grad)
        z1 = dot("tbj,jbk->tjk", v1, left_one).astype(bf)
        hidden = gelu_value(z1.astype(f32)).astype(bf)
        u2 = dot("tjk,kjm->tkm", hidden, right_two).astype(bf)
        w2 = dot("tkm,mkn->tnm", u2, left_two).astype(bf)
        dw_two, w2 = lax.optimization_barrier((dw_two, w2))
        mixed = to_blocks(w2)
        du2 = dot("tnm,mkn->tkm", dw_two, left_two).astype(bf)
        gl2 = dot("tkm,tnm->mkn", u2, dw_two)
        gr2 = dot("tjk,tkm->kjm", hidden, du2)
        dh = dot("tkm,kjm->tjk", du2, right_two)
        dz1 = (dh * gelu_slope(z1.astype(f32))).astype(bf)
        dv1 = dot("tjk,jbk->tbj", dz1, left_one).astype(bf)
        gl1 = dot("tbj,tjk->jbk", v1, dz1)
        mixed, dv1, gl2, gr2, gl1 = lax.optimization_barrier(
            (mixed, dv1, gl2.astype(bf), gr2.astype(bf), gl1.astype(bf))
        )
        du1 = to_blocks(dv1)
        gl2, gr2, gl1 = reduce_all((gl2, gr2, gl1), n_dp, n_z)
        layer_out = (tokens_in.astype(f32) + mixed.astype(f32)).astype(bf)
        gr1 = dot("tbi,tbo->bio", tokens_in, du1)
        input_grad = (out_grad.astype(f32) + dot("tbo,bio->tbi", du1, right_one)).astype(bf)
        gr1 = gr1.astype(bf).reshape(gr1.shape[0], n_dp, -1, gr1.shape[2])
        gr1 = lax.all_to_all(gr1, "dp", split_axis=1, concat_axis=1, tiled=True)
        gr1 = jnp.sum(gr1.astype(f32), axis=1)
        return (layer_out, input_grad, gr1, gl1, gr2, gl2)

    return on_device


def solution(mesh):
    split = P("dp", "tensor", None)
    factor = P("tensor", None, None)
    grad = P("tensor", "dp", None)
    return jax.shard_map(
        make(mesh.shape["dp"], mesh.shape["tensor"] // 2),
        mesh=mesh,
        in_specs=(split, factor, factor, factor, factor, split),
        out_specs=(split, split, grad, grad, grad, grad),
        check_vma=False,
    )
```
